32 devices in a mesh: macro: 8 (over z, core), cell: 4 (over y, x).
Axes of the slice: x: 2, y: 2, z: 4, core: 2. Of those that a mesh axis runs over, the one named last changes fastest.
Arguments:
- coarse_thermal_field: float32 [32, 64, 128], P('macro', 'cell'), may hold values from -6 to 6
- representative_unit_choice: int32 [32, 64, 128], P('macro', 'cell'), may hold values from 0 to 7, as said below
- inspected_fine_location: int32 [3, 32, 64, 128], P(None, 'macro', 'cell'), may hold values from 0 to 63
- void_solid_labelling: int32 [8, 64, 4096], P('macro', 'cell'), may hold values from 0 to 1, as said below
- material_conductance_pairs: float32 [8, 2], P('macro'), may hold values from 0.2 to 4
Outputs:
- flux: float32 [3, 32, 64, 128], P(None, 'macro', 'cell')
- probe_flux: float32 [3, 32, 64, 128], P(None, 'macro', 'cell')
The draws below stay inside these ranges and needn't reach their ends.
Inputs may be any that keep to these rules, and one draw needn't show every extreme that they name: Within the macro cells held by one device (4 x 16 x 128 cells, one index of macro with one index of cell), no pair of a unit cell s = representative_unit_choice and a slab inspected_fine_location[0] // 16 occurs more than 512 times, and one pair, the same for every device, occurs exactly 512 times on every device. `void_solid_labelling`: 1 marks a pore cell, 0 a solid cell.
All inputs are finite; a program needn't handle non-finite values.
Results may differ from the reference program's by a relative error of at most 0.0003.
Values sent between devices are 32-bit elements; how exact they have to be, the bound alone decides.
A program may use at most 128 MiB of HBM per device.

```python
import math
import jax
import jax.numpy as jnp
from jax import lax

MC = 64
ITERS = 2
TX = 4
TY = 16
COARSE_NUM_THIRD = 128
COARSE_NUM_FIRST = 32
COARSE_NUM_SECOND = 64
ROWS_DEV = 8192
CAP = 512
UCELLS = 8
N_MACRO = 8
N_CELL = 4


def joint_routes(key):
    base = jax.random.fold_in(key, 7)
    key_busy, key_devices, key_x, key_y, key_z = jax.random.split(base, 5)
    device_count = N_MACRO * N_CELL
    bucket_count = N_MACRO * N_CELL
    busiest = jax.random.randint(key_busy, (), 0, bucket_count)
    bucket_ids = jnp.arange(bucket_count, dtype=jnp.int32)

    def one_device(device_key):
        key_weight, key_order, key_shuffle = jax.random.split(device_key, 3)
        weights = jax.random.randint(key_weight, (bucket_count,), 2, 4)
        weights = jnp.where(bucket_ids == busiest, 0, weights)
        spare = ROWS_DEV - CAP
        shares = spare * weights // jnp.sum(weights)
        leftover = spare - jnp.sum(shares)
        ordering = jax.random.permutation(key_order, bucket_count)
        scores = jnp.where(bucket_ids == busiest, bucket_count + ordering, ordering)
        ranking = jnp.argsort(jnp.argsort(scores))
        counts = shares + (ranking < leftover).astype(jnp.int32)
        counts = jnp.where(bucket_ids == busiest, CAP, counts)
        boundary = jnp.cumsum(counts)
        positions = jnp.arange(ROWS_DEV, dtype=jnp.int32)
        labels = jnp.searchsorted(boundary, positions, side='right')
        return jax.random.permutation(key_shuffle, labels).astype(jnp.int32)
    device_maps = jax.vmap(one_device)(jax.random.split(key_devices, device_count))
    device_maps = device_maps.reshape(N_MACRO, N_CELL, TX, TY, COARSE_NUM_THIRD).transpose(0, 2, 1, 3, 4)
    labels = device_maps.reshape(COARSE_NUM_FIRST, COARSE_NUM_SECOND, COARSE_NUM_THIRD).astype(jnp.int32)
    slab_depth = MC // N_CELL
    plane_x = labels % N_CELL * slab_depth + jax.random.randint(key_x, (COARSE_NUM_FIRST, COARSE_NUM_SECOND, COARSE_NUM_THIRD), 0, slab_depth)
    plane_y = jax.random.randint(key_y, (COARSE_NUM_FIRST, COARSE_NUM_SECOND, COARSE_NUM_THIRD), 0, MC)
    plane_z = jax.random.randint(key_z, (COARSE_NUM_FIRST, COARSE_NUM_SECOND, COARSE_NUM_THIRD), 0, MC)
    return (labels // N_CELL, plane_x.astype(jnp.int32), plane_y.astype(jnp.int32), plane_z.astype(jnp.int32))


def draw_representative_unit_choice(key, part):
    routes = joint_routes(key)
    return routes[0].astype(jnp.int32)


def draw_inspected_fine_location(key, part):
    routes = joint_routes(key)
    return jnp.stack([routes[1], routes[2], routes[3]]).astype(jnp.int32)


def draw_void_solid_labelling(key, part):
    key_share, key_cells = jax.random.split(key)
    percent = jax.random.randint(key_share, (UCELLS, 1, 1), 30, 61)
    depth_index = jnp.arange(MC, dtype=jnp.int32)[None, :, None]
    threshold = percent * (MC // 2 + depth_index) // MC
    rolled = jax.random.randint(key_cells, (UCELLS, MC, MC * MC), 0, 100)
    return (rolled < threshold).astype(jnp.int32)


def shard_levels(own_key, dims, pieces, low, high):
    def one(axis_at, blocks):
        draws = jax.random.uniform(jax.random.fold_in(jax.random.fold_in(own_key, 6), axis_at), (blocks,), jnp.float32, low / len(pieces), high / len(pieces))
        return jnp.repeat(jnp.exp(draws), dims[axis_at] // blocks).reshape((-1,) + (1,) * (len(dims) - axis_at - 1))

    level = one(*pieces[0])
    for cut in pieces[1:]:
        level = level * one(*cut)
    return level


def scatter_about(stream_key, shape, scale, limit, pieces=(), kind=jnp.bfloat16):
    factor_of = shard_levels(stream_key, shape, pieces, -0.22, 0.18) if pieces else 1.0
    entries = jax.random.normal(stream_key, shape, jnp.float32) * scale * factor_of
    return jnp.minimum(jnp.maximum(entries, -limit), limit).astype(kind)


def setup_inputs(seed: int = 0) -> dict:
    arg_keys = jax.random.split(jax.random.key(seed), 6)
    coarse_thermal_field = scatter_about(arg_keys[0], (COARSE_NUM_FIRST, COARSE_NUM_SECOND, COARSE_NUM_THIRD), 1.0, 6.0, ((0, 8), (1, 4)), jnp.float32)
    representative_unit_choice = draw_representative_unit_choice(jax.random.fold_in(arg_keys[5], 71), 0)
    inspected_fine_location = draw_inspected_fine_location(jax.random.fold_in(arg_keys[5], 71), 0)
    void_solid_labelling = draw_void_solid_labelling(jax.random.fold_in(arg_keys[5], 71), 0)
    material_conductance_pairs = jnp.clip(jnp.exp(math.log(4.0) - 2.9957323 * jax.random.uniform(arg_keys[4], (UCELLS, 2), jnp.float32) ** shard_levels(arg_keys[4], (UCELLS, 2), ((0, 8),), -0.2, 0.2)), 0.2, 4.0)
    return dict(coarse_thermal_field=coarse_thermal_field, representative_unit_choice=representative_unit_choice, inspected_fine_location=inspected_fine_location, void_solid_labelling=void_solid_labelling, material_conductance_pairs=material_conductance_pairs)


def wave_numbers(length):
    grid_index = jnp.arange(length, dtype=jnp.int32)
    return jnp.where(grid_index < length // 2, grid_index, grid_index - length).astype(jnp.float32)


def cell_fields(pore_cells, conduct_pair):
    solid_k = conduct_pair[0]
    pore_k = conduct_pair[1]
    local_k = jnp.where(pore_cells.reshape(MC, MC, MC) == 1, pore_k, solid_k)
    ref_k = 0.5 * (solid_k + pore_k)
    wave_x = wave_numbers(MC)[:, None, None]
    wave_y = wave_numbers(MC)[None, :, None]
    wave_z = wave_numbers(MC)[None, None, :]
    squared = wave_x * wave_x + wave_y * wave_y + wave_z * wave_z
    factor = jnp.where(squared > 0, -1.0 / (ref_k * jnp.maximum(squared, 1.0)), 0.0)
    identity = jnp.eye(3, dtype=jnp.float32)[:, :, None, None, None]
    gradient = jnp.broadcast_to(identity, (3, 3, MC, MC, MC))
    for sweep in range(ITERS):
        polar = (local_k - ref_k) * gradient
        spectra = jnp.fft.fftn(polar, axes=(2, 3, 4))
        projected = wave_x * spectra[:, 0] + wave_y * spectra[:, 1] + wave_z * spectra[:, 2]
        response = jnp.stack([wave_x * projected * factor, wave_y * projected * factor, wave_z * projected * factor], axis=1)
        gradient = identity + jnp.fft.ifftn(response, axes=(2, 3, 4)).real
    tensor = jnp.mean(local_k * gradient, axis=(2, 3, 4)).T
    table = (-(local_k * gradient)).reshape(3, 3, MC * MC * MC)
    return tensor, table


def reference(coarse_thermal_field, representative_unit_choice, inspected_fine_location, void_solid_labelling, material_conductance_pairs):
    def per_cell(cell_pair):
        return cell_fields(cell_pair[0], cell_pair[1])

    tensors, tables = lax.map(per_cell, (void_solid_labelling, material_conductance_pairs))
    enlarged_span = jnp.pad(coarse_thermal_field, 1)
    grad_x = (enlarged_span[2:, 1:-1, 1:-1] - enlarged_span[:-2, 1:-1, 1:-1]) * 0.5
    grad_y = (enlarged_span[1:-1, 2:, 1:-1] - enlarged_span[1:-1, :-2, 1:-1]) * 0.5
    grad_z = (enlarged_span[1:-1, 1:-1, 2:] - enlarged_span[1:-1, 1:-1, :-2]) * 0.5
    components = []
    for component in range(3):
        total = tensors[:, component, 0][representative_unit_choice] * grad_x
        total = total + tensors[:, component, 1][representative_unit_choice] * grad_y
        total = total + tensors[:, component, 2][representative_unit_choice] * grad_z
        components.append(-total)
    point = (inspected_fine_location[0] * MC + inspected_fine_location[1]) * MC + inspected_fine_location[2]
    flat_index = (representative_unit_choice * (MC * MC * MC) + point).astype(jnp.int32)
    probes = []
    for component in range(3):
        total = tables[:, 0, component].reshape(-1)[flat_index] * grad_x
        total = total + tables[:, 1, component].reshape(-1)[flat_index] * grad_y
        total = total + tables[:, 2, component].reshape(-1)[flat_index] * grad_z
        probes.append(total)
    return jnp.stack(components), jnp.stack(probes)
```

```python
import functools
import math

import jax
import jax.numpy as jnp
from jax import lax
from jax.experimental import pallas as pl
from jax.experimental.pallas import tpu as pltpu
from jax.sharding import PartitionSpec as P

high = lax.Precision.HIGH
highest = lax.Precision.HIGHEST
BOTH = ("macro", "cell")


def einsum(eq, a, b):
    return jnp.einsum(eq, a, b, precision=high)


def neighbours(value, axis, dim):
    peers, length = lax.axis_size(axis), value.shape[dim]
    up = [(i, i + 1) for i in range(peers - 1)]
    down = [(i + 1, i) for i in range(peers - 1)]
    before = lax.ppermute(lax.slice_in_dim(value, length - 1, length, axis=dim), axis, up)
    after = lax.ppermute(lax.slice_in_dim(value, 0, 1, axis=dim), axis, down)
    return jnp.concatenate([before, value, after], axis=dim)


def dft_tables(length):
    grid_index = jnp.arange(length, dtype=jnp.int32)
    phases = grid_index[:, None] * grid_index[None, :] % length
    angles = phases.astype(jnp.float32) * (2.0 * math.pi / length)
    return jnp.cos(angles), jnp.sin(angles)


def wave_numbers(grid_index, length):
    return jnp.where(grid_index < length // 2, grid_index, grid_index - length).astype(jnp.float32)


def rotate(values):
    half = values.shape[-1] // 2
    return jnp.concatenate([values[..., half:], -values[..., :half]], axis=-1)


def forward(eq, cosine, sines, values):
    return einsum(eq, cosine, values) + einsum(eq, sines, rotate(values))


def inverse(eq, cosine, sines, values):
    return einsum(eq, cosine, values) - einsum(eq, sines, rotate(values))


def lookup_kernel(fields, k_ref, l_ref, table_ref, out_ref, split):
    rows, depth = table_ref.shape
    length = rows // fields
    block = k_ref.shape[1]

    @pl.when(pl.program_id(0) == 0)
    def _():
        whole = table_ref[...]
        upper = whole.astype(jnp.bfloat16)
        split[:rows] = upper
        split[rows:] = (whole - upper.astype(jnp.float32)).astype(jnp.bfloat16)

    at_k = lax.broadcasted_iota(jnp.int32, (depth, block), 0) == k_ref[...]
    picked = jnp.dot(
        split[...],
        jnp.where(at_k, 1.0, 0.0).astype(jnp.bfloat16),
        preferred_element_type=jnp.float32,
    )
    at_l = lax.broadcasted_iota(jnp.int32, (length, block), 0) == l_ref[...]
    for field in range(fields):
        first = field * length
        both = picked[first : first + length] + picked[rows + first : rows + first + length]
        out_ref[field : field + 1] = jnp.sum(jnp.where(at_l, both, 0.0), axis=0, keepdims=True)


def lookup(table, k_index, l_index, block=512):
    fields, length, depth = table.shape
    count = k_index.shape[0]
    rows = fields * length
    return pl.pallas_call(
        functools.partial(lookup_kernel, fields),
        grid=(count // block,),
        in_specs=[
            pl.BlockSpec((1, block), lambda i: (0, i)),
            pl.BlockSpec((1, block), lambda i: (0, i)),
            pl.BlockSpec((rows, depth), lambda i: (0, 0)),
        ],
        out_specs=pl.BlockSpec((fields, block), lambda i: (0, i)),
        out_shape=jax.ShapeDtypeStruct((fields, count), jnp.float32),
        scratch_shapes=[pltpu.VMEM((2 * rows, depth), jnp.bfloat16)],
        compiler_params=pltpu.CompilerParams(vmem_limit_bytes=40 * 1024 * 1024),
        cost_estimate=pl.CostEstimate(
            flops=4 * rows * depth * count, bytes_accessed=4 * rows * depth, transcendentals=0
        ),
    )(k_index.reshape(1, count), l_index.reshape(1, count), table.reshape(rows, depth))


def probe_kernel(k_ref, l_ref, along_ref, waves_ref, local_ref, out_ref, mean_ref, split):
    fields, depth = along_ref.shape[:2]
    length, block = waves_ref.shape[0], k_ref.shape[1]
    rows = fields * length

    @pl.when(pl.program_id(0) == 0)
    def _():
        local_k = local_ref[...]
        for field in range(fields):
            update = lax.dot_general(
                waves_ref[...],
                along_ref[field],
                (((1,), (1,)), ((), ())),
                precision=highest,
                preferred_element_type=jnp.float32,
            )
            unit = 1.0 if field % 4 == 0 else 0.0
            values = local_k * (update + unit)
            total = jnp.sum(jnp.sum(values, axis=0, keepdims=True), axis=1, keepdims=True)
            mean_ref[field : field + 1] = jnp.broadcast_to(total, (1, mean_ref.shape[1]))
            upper = values.astype(jnp.bfloat16)
            first = field * length
            split[first : first + length] = upper
            split[rows + first : rows + first + length] = (
                values - upper.astype(jnp.float32)
            ).astype(jnp.bfloat16)

    at_k = lax.broadcasted_iota(jnp.int32, (depth, block), 0) == k_ref[...]
    picked = jnp.dot(
        split[...],
        jnp.where(at_k, 1.0, 0.0).astype(jnp.bfloat16),
        preferred_element_type=jnp.float32,
    )
    at_l = lax.broadcasted_iota(jnp.int32, (length, block), 0) == l_ref[...]
    for field in range(fields):
        first = field * length
        both = picked[first : first + length] + picked[rows + first : rows + first + length]
        out_ref[field : field + 1] = jnp.sum(jnp.where(at_l, both, 0.0), axis=0, keepdims=True)


def probe(along, waves, local_k, k_index, l_index, block=512):
    fields, depth, width = along.shape
    length = waves.shape[0]
    count = k_index.shape[0]
    rows, lanes = fields * length, 128
    return pl.pallas_call(
        probe_kernel,
        grid=(count // block,),
        in_specs=[
            pl.BlockSpec((1, block), lambda i: (0, i)),
            pl.BlockSpec((1, block), lambda i: (0, i)),
            pl.BlockSpec((fields, depth, width), lambda i: (0, 0, 0)),
            pl.BlockSpec((length, width), lambda i: (0, 0)),
            pl.BlockSpec((length, depth), lambda i: (0, 0)),
        ],
        out_specs=[
            pl.BlockSpec((fields, block), lambda i: (0, i)),
            pl.BlockSpec((fields, lanes), lambda i: (0, 0)),
        ],
        out_shape=[
            jax.ShapeDtypeStruct((fields, count), jnp.float32),
            jax.ShapeDtypeStruct((fields, lanes), jnp.float32),
        ],
        scratch_shapes=[pltpu.VMEM((2 * rows, depth), jnp.bfloat16)],
        compiler_params=pltpu.CompilerParams(vmem_limit_bytes=40 * 1024 * 1024),
        cost_estimate=pl.CostEstimate(
            flops=4 * rows * depth * count, bytes_accessed=8 * rows * depth, transcendentals=0
        ),
    )(k_index.reshape(1, count), l_index.reshape(1, count), along, waves, local_k)


def upper_lower(values):
    upper = lax.reduce_precision(values, 8, 7)
    return upper.astype(jnp.bfloat16), (values - upper).astype(jnp.bfloat16)


def one_hot(index, count):
    return (jnp.arange(count, dtype=jnp.int32)[:, None] == index[None, :]).astype(jnp.bfloat16)


def exact_dot(eq, a, b):
    return jnp.einsum(eq, a, b, preferred_element_type=jnp.float32)


def slots_of(targets, buckets, capacity):
    count = targets.shape[0]
    lanes = 128
    marks = one_hot(targets, buckets).reshape(buckets, count // lanes, lanes)
    lane = jnp.arange(lanes)
    within = exact_dot("bij,jk->bik", marks, (lane[:, None] < lane[None, :]).astype(jnp.bfloat16))
    totals = jnp.sum(marks.astype(jnp.float32), axis=2).astype(jnp.bfloat16)
    step = jnp.arange(count // lanes)
    before = exact_dot("bi,ik->bk", totals, (step[:, None] < step[None, :]).astype(jnp.bfloat16))
    rank = jnp.sum(marks * (within + before[:, :, None]), axis=0)
    return targets * capacity + rank.reshape(count).astype(jnp.int32)


def unit_fields(labels, pair, received):
    cell_count = lax.axis_size("cell")
    here = lax.axis_index("cell")
    slab = labels.shape[1]
    length = slab * cell_count
    cosine, sines = dft_tables(length)
    grid_index = jnp.arange(length, dtype=jnp.int32)
    waves = wave_numbers(grid_index, length)
    wave_z = jnp.tile(waves, 2)
    wx, wy, wz = waves[:, None, None], waves[None, :, None], wave_z[None, None, :]
    solid_k, pore_k = pair[0, 0], pair[0, 1]
    ref_k = 0.5 * (solid_k + pore_k)
    half = 0.5 * (pore_k - solid_k)
    to_complex = jnp.concatenate([cosine, -sines], axis=1)
    to_real = jnp.concatenate([cosine, -sines], axis=0) * (1.0 / (length * length * length))

    def factor_of(squared):
        return jnp.where(squared > 0, -1.0 / (ref_k * jnp.maximum(squared, 1.0)), 0.0)

    whole = lax.all_gather(labels[0], "cell", axis=0, tiled=True)
    sign = jnp.where(whole == 1, 1.0, -1.0).reshape(length, length, length)
    own = jnp.where(labels[0] == 1, 1.0, -1.0).reshape(slab, length, length)

    spectrum = einsum("xyz,zk->xyk", sign, to_complex)
    spectrum = forward("ky,xyz->xkz", cosine, sines, spectrum)
    spectrum = forward("kx,xyz->kyz", cosine, sines, spectrum)
    base = spectrum * (factor_of(wx * wx + wy * wy + wz * wz) * half)
    powers = jnp.stack([wx * wx * base, wx * base, base])
    slab_cos = lax.dynamic_slice_in_dim(cosine, here * slab, slab, axis=0)
    slab_sin = lax.dynamic_slice_in_dim(sines, here * slab, slab, axis=0)
    two, one, zero = inverse("xk,mkyz->mxyz", slab_cos, slab_sin, powers)
    wk = waves[None, :, None]
    by_y = inverse(
        "yk,mxkz->mxyz",
        cosine,
        sines,
        jnp.stack([two, wk * one, one, wk * wk * zero, wk * zero, zero]),
    )
    ones = jnp.ones_like(wave_z)
    z_scale = jnp.stack([ones, ones, wave_z, ones, wave_z, wave_z * wave_z])
    update = einsum("mxyk,kz->mxyz", by_y * z_scale[:, None, None, :], to_real)
    unit = jnp.array([1.0, 0.0, 0.0, 1.0, 0.0, 1.0], jnp.float32)[:, None, None, None]
    polar = (own * half) * (update + unit)

    along = einsum("mxyz,zk->mxyk", polar, to_complex)
    xx, xy, xz, yy, yz, zz = forward("ky,mxyz->mkxz", cosine, sines, along)
    wk = waves[:, None, None]
    sent = jnp.stack([xx, xy, xz, wk * xy + wz * xz, wk * yy + wz * yz, wk * yz + wz * zz])
    sent, received = lax.optimization_barrier((sent, received))
    band = lax.all_to_all(sent, "cell", split_axis=1, concat_axis=2, tiled=True)
    band = forward("kx,mbxz->mbkz", cosine, sines, band)
    band_y = wave_numbers(here * slab + jnp.arange(slab, dtype=jnp.int32), length)[:, None, None]
    band_x = waves[None, :, None]
    projected = (band_x * band[:3] + band[3:]) * factor_of(
        band_x * band_x + band_y * band_y + wz * wz
    )
    back = inverse("xk,mbkz->mbxz", cosine, sines, jnp.concatenate([band_x * projected, projected]))
    back = lax.all_to_all(back, "cell", split_axis=2, concat_axis=1, tiled=True)
    rx, r1 = back[:3], back[3:]
    parts = jnp.stack([rx, wk * r1, wz * r1], axis=1).reshape(9, length, slab, 2 * length)
    along = inverse("yk,nkxz->nxyz", cosine, sines, parts)
    local_k = jnp.where(labels[0] == 1, pore_k, solid_k).reshape(slab * length, length)
    along = along.reshape(9, slab * length, 2 * length)
    return along, to_real.T, local_k.T, received


def shards(temperature, choice, location, labels, pair):
    cell_count, macro_count = lax.axis_size("cell"), lax.axis_size("macro")
    slab = labels.shape[1]
    length = slab * cell_count
    devices = macro_count * cell_count
    span = temperature.shape
    rows = span[0] * span[1] * span[2]
    capacity = 2 * rows // devices
    lanes = 128

    tall = neighbours(temperature, "macro", 0)
    wide = neighbours(temperature, "cell", 1)
    deep = jnp.pad(temperature, ((0, 0), (0, 0), (1, 1)))
    gradients = (
        jnp.stack(
            [
                tall[2:] - tall[:-2],
                wide[:, 2:] - wide[:, :-2],
                deep[:, :, 2:] - deep[:, :, :-2],
            ]
        ).reshape(3, rows)
        * 0.5
    )
    units = choice.reshape(rows)
    px, py, pz = location.reshape(3, rows)
    slots = slots_of(units * cell_count + px // slab, devices, capacity)
    offsets = ((px % slab) * length + py) * length + pz
    payload = jnp.concatenate([gradients, offsets.astype(jnp.float32)[None]])
    upper, lower = upper_lower(payload)
    slot_rows = devices * capacity // lanes
    at_row, at_lane = one_hot(slots // lanes, slot_rows), one_hot(slots % lanes, lanes)
    spread = (jnp.stack([upper, lower])[:, :, None, :] * at_row).reshape(8 * slot_rows, rows)
    placed = exact_dot("rn,ln->rl", spread, at_lane).reshape(2, 4, devices, capacity)
    outgoing = (placed[0] + placed[1]).transpose(1, 0, 2)
    received = lax.all_to_all(outgoing, BOTH, split_axis=0, concat_axis=0, tiled=True)
    along, waves, local_k, received = unit_fields(labels, pair, received)
    received = received.transpose(1, 0, 2).reshape(4, devices * capacity)
    got_offset = received[3].astype(jnp.int32)
    found, sums = probe(along, waves, local_k, got_offset // length, got_offset % length)
    found = found.reshape(3, 3, devices * capacity)
    answers = -jnp.sum(found * received[:3, None, :], axis=0)
    answers = answers.reshape(3, devices, capacity).transpose(1, 0, 2)
    shares = jnp.pad(sums[:, 0] / (length * length * length), (0, lanes - 9))
    answers = jnp.concatenate(
        [
            answers.reshape(devices, 3 * capacity),
            jnp.broadcast_to(shares[None, :], (devices, lanes)),
        ],
        axis=1,
    )
    returned = lax.all_to_all(answers, BOTH, split_axis=0, concat_axis=0, tiled=True)
    shares = returned[:, 3 * capacity : 3 * capacity + 9]
    tensors = jnp.sum(shares.reshape(macro_count, cell_count, 9), axis=1).T
    returned = returned[:, : 3 * capacity].reshape(devices, 3, capacity)
    returned = returned.transpose(1, 0, 2).reshape(3, slot_rows, lanes)
    probes = lookup(returned, slots % lanes, slots // lanes)

    marks = (jnp.arange(macro_count)[:, None] == units[None, :]).astype(jnp.float32)
    chosen = jnp.einsum("tu,un->tn", tensors, marks, precision=highest).reshape(3, 3, rows)
    flux = -jnp.sum(chosen * gradients[:, None, :], axis=0)
    return flux.reshape((3,) + span), probes.reshape((3,) + span)


def solution(mesh):
    in_specs = (
        P("macro", "cell", None),
        P("macro", "cell", None),
        P(None, "macro", "cell", None),
        P("macro", "cell", None),
        P("macro", None),
    )
    out_specs = (P(None, "macro", "cell", None), P(None, "macro", "cell", None))
    return jax.shard_map(shards, mesh=mesh, in_specs=in_specs, out_specs=out_specs, check_vma=False)
```

```python
import functools
import math

import jax
import jax.numpy as jnp
from jax import lax
from jax.experimental import pallas as pl
from jax.experimental.pallas import tpu as pltpu
from jax.sharding import PartitionSpec as P

high = lax.Precision.HIGH
highest = lax.Precision.HIGHEST
BOTH = ("macro", "cell")


def einsum(eq, a, b):
    return jnp.einsum(eq, a, b, precision=high)


def neighbours(value, axis, dim):
    peers, length = lax.axis_size(axis), value.shape[dim]
    up = [(i, i + 1) for i in range(peers - 1)]
    down = [(i + 1, i) for i in range(peers - 1)]
    before = lax.ppermute(lax.slice_in_dim(value, length - 1, length, axis=dim), axis, up)
    after = lax.ppermute(lax.slice_in_dim(value, 0, 1, axis=dim), axis, down)
    return jnp.concatenate([before, value, after], axis=dim)


def dft_tables(length):
    grid_index = jnp.arange(length, dtype=jnp.int32)
    phases = grid_index[:, None] * grid_index[None, :] % length
    angles = phases.astype(jnp.float32) * (2.0 * math.pi / length)
    return jnp.cos(angles), jnp.sin(angles)


def wave_numbers(grid_index, length):
    return jnp.where(grid_index < length // 2, grid_index, grid_index - length).astype(jnp.float32)


def rotate(values):
    half = values.shape[-1] // 2
    return jnp.concatenate([values[..., half:], -values[..., :half]], axis=-1)


def forward(eq, cosine, sines, values):
    return einsum(eq, cosine, values) + einsum(eq, sines, rotate(values))


def inverse(eq, cosine, sines, values):
    return einsum(eq, cosine, values) - einsum(eq, sines, rotate(values))


def lookup_kernel(fields, k_ref, l_ref, table_ref, out_ref, split):
    rows, depth = table_ref.shape
    length = rows // fields
    block = k_ref.shape[1]

    @pl.when(pl.program_id(0) == 0)
    def _():
        whole = table_ref[...]
        upper = whole.astype(jnp.bfloat16)
        split[:rows] = upper
        split[rows:] = (whole - upper.astype(jnp.float32)).astype(jnp.bfloat16)

    at_k = lax.broadcasted_iota(jnp.int32, (depth, block), 0) == k_ref[...]
    picked = jnp.dot(
        split[...],
        jnp.where(at_k, 1.0, 0.0).astype(jnp.bfloat16),
        preferred_element_type=jnp.float32,
    )
    at_l = lax.broadcasted_iota(jnp.int32, (length, block), 0) == l_ref[...]
    for field in range(fields):
        first = field * length
        both = picked[first : first + length] + picked[rows + first : rows + first + length]
        out_ref[field : field + 1] = jnp.sum(jnp.where(at_l, both, 0.0), axis=0, keepdims=True)


def lookup(table, k_index, l_index, block=512):
    fields, length, depth = table.shape
    count = k_index.shape[0]
    rows = fields * length
    return pl.pallas_call(
        functools.partial(lookup_kernel, fields),
        grid=(count // block,),
        in_specs=[
            pl.BlockSpec((1, block), lambda i: (0, i)),
            pl.BlockSpec((1, block), lambda i: (0, i)),
            pl.BlockSpec((rows, depth), lambda i: (0, 0)),
        ],
        out_specs=pl.BlockSpec((fields, block), lambda i: (0, i)),
        out_shape=jax.ShapeDtypeStruct((fields, count), jnp.float32),
        scratch_shapes=[pltpu.VMEM((2 * rows, depth), jnp.bfloat16)],
        compiler_params=pltpu.CompilerParams(vmem_limit_bytes=40 * 1024 * 1024),
        cost_estimate=pl.CostEstimate(
            flops=4 * rows * depth * count, bytes_accessed=4 * rows * depth, transcendentals=0
        ),
    )(k_index.reshape(1, count), l_index.reshape(1, count), table.reshape(rows, depth))


def probe_kernel(k_ref, l_ref, along_ref, waves_ref, local_ref, out_ref, mean_ref, split):
    fields, depth = along_ref.shape[:2]
    length, block = waves_ref.shape[0], k_ref.shape[1]
    rows = fields * length

    @pl.when(pl.program_id(0) == 0)
    def _():
        local_k = local_ref[...]
        for field in range(fields):
            update = lax.dot_general(
                waves_ref[...],
                along_ref[field],
                (((1,), (1,)), ((), ())),
                precision=highest,
                preferred_element_type=jnp.float32,
            )
            unit = 1.0 if field % 4 == 0 else 0.0
            values = local_k * (update + unit)
            total = jnp.sum(jnp.sum(values, axis=0, keepdims=True), axis=1, keepdims=True)
            mean_ref[field : field + 1] = jnp.broadcast_to(total, (1, mean_ref.shape[1]))
            upper = values.astype(jnp.bfloat16)
            first = field * length
            split[first : first + length] = upper
            split[rows + first : rows + first + length] = (
                values - upper.astype(jnp.float32)
            ).astype(jnp.bfloat16)

    at_k = lax.broadcasted_iota(jnp.int32, (depth, block), 0) == k_ref[...]
    picked = jnp.dot(
        split[...],
        jnp.where(at_k, 1.0, 0.0).astype(jnp.bfloat16),
        preferred_element_type=jnp.float32,
    )
    at_l = lax.broadcasted_iota(jnp.int32, (length, block), 0) == l_ref[...]
    for field in range(fields):
        first = field * length
        both = picked[first : first + length] + picked[rows + first : rows + first + length]
        out_ref[field : field + 1] = jnp.sum(jnp.where(at_l, both, 0.0), axis=0, keepdims=True)


def probe(along, waves, local_k, k_index, l_index, block=512):
    fields, depth, width = along.shape
    length = waves.shape[0]
    count = k_index.shape[0]
    rows, lanes = fields * length, 128
    return pl.pallas_call(
        probe_kernel,
        grid=(count // block,),
        in_specs=[
            pl.BlockSpec((1, block), lambda i: (0, i)),
            pl.BlockSpec((1, block), lambda i: (0, i)),
            pl.BlockSpec((fields, depth, width), lambda i: (0, 0, 0)),
            pl.BlockSpec((length, width), lambda i: (0, 0)),
            pl.BlockSpec((length, depth), lambda i: (0, 0)),
        ],
        out_specs=[
            pl.BlockSpec((fields, block), lambda i: (0, i)),
            pl.BlockSpec((fields, lanes), lambda i: (0, 0)),
        ],
        out_shape=[
            jax.ShapeDtypeStruct((fields, count), jnp.float32),
            jax.ShapeDtypeStruct((fields, lanes), jnp.float32),
        ],
        scratch_shapes=[pltpu.VMEM((2 * rows, depth), jnp.bfloat16)],
        compiler_params=pltpu.CompilerParams(vmem_limit_bytes=40 * 1024 * 1024),
        cost_estimate=pl.CostEstimate(
            flops=4 * rows * depth * count, bytes_accessed=8 * rows * depth, transcendentals=0
        ),
    )(k_index.reshape(1, count), l_index.reshape(1, count), along, waves, local_k)


def upper_lower(values):
    upper = lax.reduce_precision(values, 8, 7)
    return upper.astype(jnp.bfloat16), (values - upper).astype(jnp.bfloat16)


def one_hot(index, count):
    return (jnp.arange(count, dtype=jnp.int32)[:, None] == index[None, :]).astype(jnp.bfloat16)


def exact_dot(eq, a, b):
    return jnp.einsum(eq, a, b, preferred_element_type=jnp.float32)


def slots_of(targets, buckets, capacity):
    count = targets.shape[0]
    lanes = 128
    marks = one_hot(targets, buckets).reshape(buckets, count // lanes, lanes)
    lane = jnp.arange(lanes)
    within = exact_dot("bij,jk->bik", marks, (lane[:, None] < lane[None, :]).astype(jnp.bfloat16))
    totals = jnp.sum(marks.astype(jnp.float32), axis=2).astype(jnp.bfloat16)
    step = jnp.arange(count // lanes)
    before = exact_dot("bi,ik->bk", totals, (step[:, None] < step[None, :]).astype(jnp.bfloat16))
    rank = jnp.sum(marks * (within + before[:, :, None]), axis=0)
    return targets * capacity + rank.reshape(count).astype(jnp.int32)


def unit_fields(labels, pair, received):
    cell_count = lax.axis_size("cell")
    here = lax.axis_index("cell")
    slab = labels.shape[1]
    length = slab * cell_count
    cosine, sines = dft_tables(length)
    grid_index = jnp.arange(length, dtype=jnp.int32)
    waves = wave_numbers(grid_index, length)
    wave_z = jnp.tile(waves, 2)
    wx, wy, wz = waves[:, None, None], waves[None, :, None], wave_z[None, None, :]
    solid_k, pore_k = pair[0, 0], pair[0, 1]
    ref_k = 0.5 * (solid_k + pore_k)
    half = 0.5 * (pore_k - solid_k)
    to_complex = jnp.concatenate([cosine, -sines], axis=1)
    to_real = jnp.concatenate([cosine, -sines], axis=0) * (1.0 / (length * length * length))

    def factor_of(squared):
        return jnp.where(squared > 0, -1.0 / (ref_k * jnp.maximum(squared, 1.0)), 0.0)

    whole = lax.all_gather(labels[0], "cell", axis=0, tiled=True)
    sign = jnp.where(whole == 1, 1.0, -1.0).reshape(length, length, length)
    own = jnp.where(labels[0] == 1, 1.0, -1.0).reshape(slab, length, length)

    spectrum = einsum("xyz,zk->xyk", sign, to_complex)
    spectrum = forward("ky,xyz->xkz", cosine, sines, spectrum)
    spectrum = forward("kx,xyz->kyz", cosine, sines, spectrum)
    base = spectrum * (factor_of(wx * wx + wy * wy + wz * wz) * half)
    slab_cos = lax.dynamic_slice_in_dim(cosine, here * slab, slab, axis=0)
    slab_sin = lax.dynamic_slice_in_dim(sines, here * slab, slab, axis=0)
    powers = jnp.stack([waves * waves, waves, jnp.ones_like(waves)])[:, None, :]
    scaled_cos = (powers * slab_cos).reshape(3 * slab, length)
    scaled_sin = (powers * slab_sin).reshape(3 * slab, length)
    scaled = inverse("xk,kyz->xyz", scaled_cos, scaled_sin, base)
    two, one, zero = scaled.reshape(3, slab, length, 2 * length)
    wk = waves[None, :, None]
    by_y = inverse(
        "yk,mxkz->mxyz",
        cosine,
        sines,
        jnp.stack([two, wk * one, one, wk * wk * zero, wk * zero, zero]),
    )
    ones = jnp.ones_like(wave_z)
    z_scale = jnp.stack([ones, ones, wave_z, ones, wave_z, wave_z * wave_z])
    update = einsum("mxyk,kz->mxyz", by_y * z_scale[:, None, None, :], to_real)
    unit = jnp.array([1.0, 0.0, 0.0, 1.0, 0.0, 1.0], jnp.float32)[:, None, None, None]
    polar = (own * half) * (update + unit)

    along = einsum("mxyz,zk->mxyk", polar, to_complex)
    xx, xy, xz, yy, yz, zz = forward("ky,mxyz->mkxz", cosine, sines, along)
    wk = waves[:, None, None]
    sent = jnp.stack([xx, xy, xz, wk * xy + wz * xz, wk * yy + wz * yz, wk * yz + wz * zz])
    sent, received = lax.optimization_barrier((sent, received))
    band = lax.all_to_all(sent, "cell", split_axis=1, concat_axis=2, tiled=True)
    band = forward("kx,mbxz->mbkz", cosine, sines, band)
    band_y = wave_numbers(here * slab + jnp.arange(slab, dtype=jnp.int32), length)[:, None, None]
    band_x = waves[None, :, None]
    projected = (band_x * band[:3] + band[3:]) * factor_of(
        band_x * band_x + band_y * band_y + wz * wz
    )
    back = inverse("xk,mbkz->mbxz", cosine, sines, jnp.concatenate([band_x * projected, projected]))
    back = lax.all_to_all(back, "cell", split_axis=2, concat_axis=1, tiled=True)
    rx, r1 = back[:3], back[3:]
    parts = jnp.stack([rx, wk * r1, wz * r1], axis=1).reshape(9, length, slab, 2 * length)
    along = inverse("yk,nkxz->nxyz", cosine, sines, parts)
    local_k = jnp.where(labels[0] == 1, pore_k, solid_k).reshape(slab * length, length)
    along = along.reshape(9, slab * length, 2 * length)
    return along, to_real.T, local_k.T, received


def shards(temperature, choice, location, labels, pair):
    cell_count, macro_count = lax.axis_size("cell"), lax.axis_size("macro")
    slab = labels.shape[1]
    length = slab * cell_count
    devices = macro_count * cell_count
    span = temperature.shape
    rows = span[0] * span[1] * span[2]
    capacity = 2 * rows // devices
    lanes = 128

    tall = neighbours(temperature, "macro", 0)
    wide = neighbours(temperature, "cell", 1)
    deep = jnp.pad(temperature, ((0, 0), (0, 0), (1, 1)))
    gradients = (
        jnp.stack(
            [
                tall[2:] - tall[:-2],
                wide[:, 2:] - wide[:, :-2],
                deep[:, :, 2:] - deep[:, :, :-2],
            ]
        ).reshape(3, rows)
        * 0.5
    )
    units = choice.reshape(rows)
    px, py, pz = location.reshape(3, rows)
    slots = slots_of(units * cell_count + px // slab, devices, capacity)
    offsets = ((px % slab) * length + py) * length + pz
    payload = jnp.concatenate([gradients, offsets.astype(jnp.float32)[None]])
    upper, lower = upper_lower(payload)
    slot_rows = devices * capacity // lanes
    at_row, at_lane = one_hot(slots // lanes, slot_rows), one_hot(slots % lanes, lanes)
    spread = (jnp.stack([upper, lower])[:, :, None, :] * at_row).reshape(8 * slot_rows, rows)
    placed = exact_dot("rn,ln->rl", spread, at_lane).reshape(2, 4, devices, capacity)
    outgoing = (placed[0] + placed[1]).transpose(1, 0, 2)
    received = lax.all_to_all(outgoing, BOTH, split_axis=0, concat_axis=0, tiled=True)
    along, waves, local_k, received = unit_fields(labels, pair, received)
    received = received.transpose(1, 0, 2).reshape(4, devices * capacity)
    got_offset = received[3].astype(jnp.int32)
    found, sums = probe(along, waves, local_k, got_offset // length, got_offset % length)
    found = found.reshape(3, 3, devices * capacity)
    answers = -jnp.sum(found * received[:3, None, :], axis=0)
    answers = answers.reshape(3, devices, capacity).transpose(1, 0, 2)
    shares = jnp.pad(sums[:, 0] / (length * length * length), (0, lanes - 9))
    answers = jnp.concatenate(
        [
            answers.reshape(devices, 3 * capacity),
            jnp.broadcast_to(shares[None, :], (devices, lanes)),
        ],
        axis=1,
    )
    returned = lax.all_to_all(answers, BOTH, split_axis=0, concat_axis=0, tiled=True)
    shares = returned[:, 3 * capacity : 3 * capacity + 9]
    tensors = jnp.sum(shares.reshape(macro_count, cell_count, 9), axis=1).T
    returned = returned[:, : 3 * capacity].reshape(devices, 3, capacity)
    returned = returned.transpose(1, 0, 2).reshape(3, slot_rows, lanes)
    probes = lookup(returned, slots % lanes, slots // lanes)

    marks = (jnp.arange(macro_count)[:, None] == units[None, :]).astype(jnp.float32)
    chosen = jnp.einsum("tu,un->tn", tensors, marks, precision=highest).reshape(3, 3, rows)
    flux = -jnp.sum(chosen * gradients[:, None, :], axis=0)
    return flux.reshape((3,) + span), probes.reshape((3,) + span)


def solution(mesh):
    in_specs = (
        P("macro", "cell", None),
        P("macro", "cell", None),
        P(None, "macro", "cell", None),
        P("macro", "cell", None),
        P("macro", None),
    )
    out_specs = (P(None, "macro", "cell", None), P(None, "macro", "cell", None))
    return jax.shard_map(shards, mesh=mesh, in_specs=in_specs, out_specs=out_specs, check_vma=False)
```
